32 devices in a mesh: groups: 2 (over y), bead: 4 (over z), space: 4 (over x, core).
Axes of the slice: x: 2, y: 2, z: 4, core: 2. Of those that a mesh axis runs over, the one named last changes fastest.
Arguments:
- positions: float32 [8, 3, 96, 128], P(('groups', 'bead'), None, 'space'), parts along dimension 0, may hold values from -5 to 5
- momenta: float32 [8, 3, 96, 128], P(('groups', 'bead'), None, 'space'), parts along dimension 0, may hold values from -6 to 6
- forces: float32 [8, 3, 96, 128], P(('groups', 'bead'), None, 'space'), parts along dimension 0, may hold values from -6 to 6
- noise: float32 [8, 3, 96, 128], P(('groups', 'bead'), None, 'space'), parts along dimension 0, may hold values from -5 to 5
- masses: float32 [192, 128], P(('groups', 'space')), parts along dimension 0, may hold values from 1 to 16
- strengths: float32 [192, 128], P(('groups', 'space')), parts along dimension 0, may hold values from 0.5 to 2
- cell_counts: int32 [192], P('groups'), parts along dimension 0, may hold values from 32 to 128, as said below
- neighbour_cells: int32 [192, 26], P(('groups', 'space')), parts along dimension 0, may hold values from -1 to 95, as said below
Outputs:
- positions_next: float32 [8, 3, 96, 128], P(('groups', 'bead'), None, 'space'), parts along dimension 0
- momenta_next: float32 [8, 3, 96, 128], P(('groups', 'bead'), None, 'space'), parts along dimension 0
- forces_next: float32 [8, 3, 96, 128], P(('groups', 'bead'), None, 'space'), parts along dimension 0
The draws below stay inside these ranges and needn't reach their ends.
There are 2 independent parts, one for each index of `groups`. The reference program is written for one: setup_inputs(seed, part) draws one part's arguments, and reference() takes and returns one part's arrays. A program takes and returns all parts, laid end to end along the dimension named above; each array names one. Nothing has to cross between parts.
Inputs may be any that keep to these rules, and one draw needn't show every extreme that they name: `neighbour_cells`: row c lists 26 different cells c + d with 0 < |d| <= 16, always c - 1 and c + 1 among them; an entry is -1 where c + d lies outside the system's cells. `cell_counts`: A cell's atoms fill its first slots; some cell of each system is full.
All inputs are finite; a program needn't handle non-finite values.
Results may differ from the reference program's by a relative error of at most 0.0003.
Values sent between devices are 32-bit elements; how exact they have to be, the bound alone decides.
A program may use at most 64 MiB of HBM per device.

```python
import math
import jax
import jax.numpy as jnp
import numpy as np
from jax import lax

CAP = 128
HALO = 16
NEIGH = 26
NBEADS = 4
CELLS = 96


def draw_cell_counts(key, part):
    first_key, second_key = jax.random.split(key)
    counts = jax.random.randint(first_key, (CELLS,), CAP // 4, CAP + 1)
    chosen = jax.random.randint(second_key, (), 0, CELLS)
    return counts.at[chosen].set(CAP).astype(jnp.int32)


def draw_neighbour_cells(key, part):
    candidates = jnp.array(np.array([step for step in range(-HALO, HALO + 1) if abs(step) > 1], dtype=np.int32))
    width_all = 2 * HALO - 2
    scores = jax.random.randint(key, (CELLS, width_all), 0, 1 << 20) * width_all + jnp.arange(width_all, dtype=jnp.int32)[None, :]
    order = jnp.argsort(scores, axis=1)[:, :NEIGH - 2]
    chosen = candidates[order]
    nearest = jnp.tile(jnp.array([[-1, 1]], dtype=jnp.int32), (CELLS, 1))
    offsets = jnp.concatenate([nearest, chosen], axis=1)
    target = jnp.arange(CELLS, dtype=jnp.int32)[:, None] + offsets
    return jnp.where((target >= 0) & (target < CELLS), target, -1).astype(jnp.int32)


def block_levels(key, extent, pieces, least, top_value):
    factor_of, own = 1.0, jax.random.fold_in(key, 6)
    for position, shards_of in pieces:
        draws = jnp.exp(jax.random.uniform(jax.random.fold_in(own, position), (shards_of,), jnp.float32, least / len(pieces), top_value / len(pieces)))
        factor_of = factor_of * jnp.repeat(draws, extent[position] // shards_of).reshape([-1 if axis == position else 1 for axis in range(len(extent))])
    return factor_of


def gaussian(key, dims, deviation, most, pieces=(), held_as=jnp.bfloat16):
    drawn = deviation * jax.random.normal(key, dims, jnp.float32)
    if pieces:
        drawn = drawn * block_levels(key, dims, pieces, -0.22, 0.18)
    return jnp.clip(drawn, -most, most).astype(held_as)


def setup_inputs(seed: int = 0, part: int = 0) -> dict:
    splits = jax.random.split(jax.random.key(seed), 9)
    own_keys = jax.random.split(jax.random.fold_in(splits[8], part), 9)
    positions = gaussian(own_keys[0], (NBEADS, 3, CELLS, CAP), 1.0, 5.0, ((0, 4), (2, 4)), jnp.float32)
    momenta = gaussian(own_keys[1], (NBEADS, 3, CELLS, CAP), 1.0, 6.0, ((0, 4), (2, 4)), jnp.float32)
    forces = gaussian(own_keys[2], (NBEADS, 3, CELLS, CAP), 1.0, 6.0, ((0, 4), (2, 4)), jnp.float32)
    noise = gaussian(own_keys[3], (NBEADS, 3, CELLS, CAP), 1.0, 5.0, ((0, 4), (2, 4)), jnp.float32)
    masses = jnp.clip(jnp.exp(math.log(16.0) - 2.7725887 * jax.random.uniform(own_keys[4], (CELLS, CAP), jnp.float32) ** block_levels(own_keys[4], (CELLS, CAP), ((0, 4),), -0.2, 0.2)), 1.0, 16.0)
    strengths = jnp.clip(jnp.exp(math.log(2.0) - 1.3862944 * jax.random.uniform(own_keys[5], (CELLS, CAP), jnp.float32) ** block_levels(own_keys[5], (CELLS, CAP), ((0, 4),), -0.2, 0.2)), 0.5, 2.0)
    cell_counts = draw_cell_counts(jax.random.fold_in(jax.random.fold_in(splits[8], part), 71), part)
    neighbour_cells = draw_neighbour_cells(jax.random.fold_in(jax.random.fold_in(splits[8], part), 71), part)
    return {"positions": positions, "momenta": momenta, "forces": forces, "noise": noise, "masses": masses, "strengths": strengths, "cell_counts": cell_counts, "neighbour_cells": neighbour_cells}


TIME_STEP = 0.5
CYCLE_FREQ = 1.5
GAMMA_ZERO = 0.5
PAIR_SCALE = 0.005

def modes_table(beads):
    rowsk = jnp.arange(beads, dtype=jnp.int32)[:, None]
    colsj = jnp.arange(beads, dtype=jnp.int32)[None, :]
    angle = 2.0 * jnp.pi * (rowsk * colsj % beads).astype(jnp.float32) / beads
    parity = jnp.where(colsj % 2 == 0, 1.0, -1.0).astype(jnp.float32)
    factor = jnp.sqrt(2.0 / beads)
    plain = jnp.ones_like(angle) / jnp.sqrt(1.0 * beads)
    table = jnp.where(rowsk == 0, plain, jnp.where(rowsk < beads // 2, factor * jnp.cos(angle), jnp.where(rowsk == beads // 2, parity * plain, factor * jnp.sin(angle))))
    return table.astype(jnp.float32)

def evolve(coords, moment, modeval, masses_here, kicks, beads):
    freq = 2.0 * CYCLE_FREQ * jnp.sin(jnp.pi * modeval / beads)
    half_step = 0.25 * TIME_STEP * 2.0
    centroid = modeval == 0.0
    cosine = jnp.cos(freq * half_step)
    sine_part = jnp.sin(freq * half_step)
    reach_term = jnp.where(centroid, half_step, sine_part / jnp.where(centroid, 1.0, freq))

    def rotate(coord_in, moment_in):
        return (cosine * coord_in + reach_term / masses_here * moment_in, -masses_here * freq * sine_part * coord_in + cosine * moment_in)
    coords, moment = rotate(coords, moment)
    damping = jnp.exp(-jnp.where(centroid, GAMMA_ZERO, 2.0 * freq) * TIME_STEP)
    moment = damping * moment + jnp.sqrt(1.0 - damping * damping) * jnp.sqrt(masses_here) * kicks
    return rotate(coords, moment)

def cell_force(own_coords, own_weight, far_coords, far_weight):
    distance = lax.optimization_barrier(jnp.sum((own_coords[:, :, None, None] - far_coords[:, None, :, :]) ** 2, axis=0))
    kernel = PAIR_SCALE * own_weight[:, None, None] * far_weight[None, :, :] * jnp.exp(-0.5 * distance)
    total = lax.optimization_barrier(jnp.sum(kernel, axis=(1, 2)))
    slots = own_coords.shape[1]
    pulled = jnp.dot(kernel.reshape(slots, -1), far_coords.reshape(3, -1).T, precision=lax.Precision.HIGHEST)
    return own_coords * total[None, :] - pulled.T

def bead_forces(coords, weights, neighbour_cells):
    ncells = coords.shape[1]
    partners = jnp.concatenate([jnp.arange(ncells, dtype=jnp.int32)[:, None], neighbour_cells], axis=1)

    def one_cell(pair):
        cell_index, plist = pair
        usable = (plist >= 0).astype(jnp.float32)
        index_list = jnp.maximum(plist, 0)
        far_coords = coords[:, index_list]
        far_weight = weights[index_list] * usable[:, None]
        return cell_force(coords[:, cell_index], weights[cell_index], far_coords, far_weight)
    result = lax.map(one_cell, (jnp.arange(ncells, dtype=jnp.int32), partners))
    return jnp.transpose(result, (1, 0, 2))

def reference(positions, momenta, forces, noise, masses, strengths, cell_counts, neighbour_cells):
    beads = positions.shape[0]
    slots = positions.shape[3]
    table = modes_table(beads)
    moment_half = momenta + 0.25 * forces
    mode_coords = jnp.einsum('kj,jxcs->kxcs', table, positions, precision=lax.Precision.HIGHEST)
    mode_moment = jnp.einsum('kj,jxcs->kxcs', table, moment_half, precision=lax.Precision.HIGHEST)
    modeval = jnp.arange(beads, dtype=jnp.float32)[:, None, None, None]
    new_coords, new_moment = evolve(mode_coords, mode_moment, modeval, masses[None, None], noise, beads)
    positions_next = jnp.einsum('kj,kxcs->jxcs', table, new_coords, precision=lax.Precision.HIGHEST)
    moved_moment = jnp.einsum('kj,kxcs->jxcs', table, new_moment, precision=lax.Precision.HIGHEST)
    live = (jnp.arange(slots, dtype=jnp.int32)[None, :] < cell_counts[:, None]).astype(jnp.float32)
    weights = strengths * live
    forces_next = lax.map(lambda coords: bead_forces(coords, weights, neighbour_cells), positions_next)
    momenta_next = moved_moment + 0.25 * forces_next
    return (positions_next, momenta_next, forces_next)
```

```python
import functools
import math

import jax
import jax.numpy as jnp
import numpy as np
from jax import lax
from jax.experimental import pallas as pl
from jax.experimental.pallas import tpu as pltpu
from jax.sharding import PartitionSpec as P

HALO = 16
TIME_STEP = 0.5
CYCLE_FREQ = 1.5
GAMMA_ZERO = 0.5
PAIR_SCALE = 0.005
ROOT = math.sqrt(math.log2(math.e))
MESH = pl.DeviceIdType.MESH


def modes_table(beads):
    k = np.arange(beads)[:, None]
    j = np.arange(beads)[None, :]
    angle = 2.0 * np.pi * (k * j % beads) / beads
    parity = np.where(j % 2 == 0, 1.0, -1.0)
    plain = np.ones_like(angle) / np.sqrt(beads)
    factor = np.sqrt(2.0 / beads)
    return np.where(
        k == 0,
        plain,
        np.where(
            k < beads // 2,
            factor * np.cos(angle),
            np.where(k == beads // 2, parity * plain, factor * np.sin(angle)),
        ),
    )


def propagator(beads):
    table = modes_table(beads)
    k = np.arange(beads)
    freq = 2.0 * CYCLE_FREQ * np.sin(np.pi * k / beads)
    half = 0.5 * TIME_STEP
    cos, sin = np.cos(freq * half), np.sin(freq * half)
    reach = np.where(k == 0, half, sin / np.where(k == 0, 1.0, freq))
    damp = np.exp(-np.where(k == 0, GAMMA_ZERO, 2.0 * freq) * TIME_STEP)
    kick = np.sqrt(1.0 - damp * damp)
    pull = -freq * sin
    modes = {
        "qq": cos * cos + reach * damp * pull,
        "qp": reach * cos * (1.0 + damp),
        "pq": pull * cos * (1.0 + damp),
        "pp": pull * reach + cos * cos * damp,
    }
    by_offset = {
        name: [float(np.sum(value * table[:, 0] * table[:, d])) for d in range(beads)]
        for name, value in modes.items()
    }
    noise = np.stack([(reach * kick)[:, None] * table, (cos * kick)[:, None] * table])
    return by_offset, noise.astype(np.float32)


def split3(value):
    high = value.astype(jnp.bfloat16).astype(jnp.float32)
    rest = value - high
    mid = rest.astype(jnp.bfloat16).astype(jnp.float32)
    return high, mid, rest - mid


def kernel(
    beads,
    spaces,
    coef,
    kicks_ref,
    counts_ref,
    list_ref,
    pos_ref,
    mom_ref,
    frc_ref,
    noi_ref,
    mass_ref,
    str_ref,
    pos_out,
    mom_out,
    frc_out,
    send_q,
    send_p,
    recv_q,
    recv_p,
    own_r,
    own_w,
    low_r,
    low_w,
    high_r,
    high_w,
    rows_v,
    rows_u,
    rows_w,
    far_b,
    far_r,
    rows_f,
    sq_sem,
    rq_sem,
    sp_sem,
    rp_sem,
    halo_send,
    halo_recv,
):
    bead = lax.axis_index("bead")
    space = lax.axis_index("space")
    cells, slots = mass_ref.shape
    neigh = list_ref.shape[1]
    wide = cells + 2 * HALO
    has_low = space > 0
    has_high = space < spaces - 1

    barrier = pltpu.get_barrier_semaphore()
    for d in range(1, beads):
        pl.semaphore_signal(
            barrier, inc=1, device_id={"bead": lax.rem(bead + d, beads)}, device_id_type=MESH
        )

    @pl.when(has_low)
    def _():
        pl.semaphore_signal(barrier, inc=1, device_id={"space": space - 1}, device_id_type=MESH)

    @pl.when(has_high)
    def _():
        pl.semaphore_signal(barrier, inc=1, device_id={"space": space + 1}, device_id_type=MESH)

    mass = mass_ref[...][None]
    root_mass = jnp.sqrt(mass)
    q = pos_ref[...]
    p = mom_ref[...] + 0.25 * frc_ref[...]
    scaled_p = p / mass
    noise_q = noi_ref[...] / root_mass
    for d in range(beads):
        target = lax.rem(bead + d, beads)
        send_q[d] = coef["qq"][d] * q + coef["qp"][d] * scaled_p + kicks_ref[0, bead, target] * noise_q

    lane = lax.broadcasted_iota(jnp.int32, (1, slots), 1)
    for c in range(cells):
        count = counts_ref[space * cells + c]
        own_w[c : c + 1, :] = jnp.where(lane < count, str_ref[c : c + 1, :], 0.0)

    pl.semaphore_wait(
        barrier, beads - 1 + has_low.astype(jnp.int32) + has_high.astype(jnp.int32)
    )

    def bead_copy(source, target, send, recv, d):
        return pltpu.make_async_remote_copy(
            src_ref=source.at[d],
            dst_ref=target.at[d],
            send_sem=send.at[d],
            recv_sem=recv.at[d],
            device_id={"bead": lax.rem(bead + d, beads)},
            device_id_type=MESH,
        )

    def space_copy(source, target, index, peer):
        return pltpu.make_async_remote_copy(
            src_ref=source,
            dst_ref=target,
            send_sem=halo_send.at[index],
            recv_sem=halo_recv.at[index],
            device_id={"space": peer},
            device_id_type=MESH,
        )

    first = pl.ds(0, HALO)
    last = pl.ds(cells - HALO, HALO)
    up_w = space_copy(own_w.at[last], low_w, 0, space + 1)
    down_w = space_copy(own_w.at[first], high_w, 1, space - 1)
    up_r = space_copy(own_r.at[:, last], low_r, 2, space + 1)
    down_r = space_copy(own_r.at[:, first], high_r, 3, space - 1)
    copies_q = [bead_copy(send_q, recv_q, sq_sem, rq_sem, d) for d in range(1, beads)]
    copies_p = [bead_copy(send_p, recv_p, sp_sem, rp_sem, d) for d in range(1, beads)]
    for copy in copies_q:
        copy.start()

    @pl.when(has_high)
    def _():
        up_w.start()

    @pl.when(has_low)
    def _():
        down_w.start()

    mass_q = mass * q
    noise_p = noi_ref[...] * root_mass
    for d in range(beads):
        target = lax.rem(bead + d, beads)
        send_p[d] = coef["pq"][d] * mass_q + coef["pp"][d] * p + kicks_ref[1, bead, target] * noise_p
    for copy in copies_p:
        copy.start()

    @pl.when(jnp.logical_not(has_low))
    def _():
        low_r[...] = jnp.zeros_like(low_r)
        low_w[...] = jnp.zeros_like(low_w)

    @pl.when(jnp.logical_not(has_high))
    def _():
        high_r[...] = jnp.zeros_like(high_r)
        high_w[...] = jnp.zeros_like(high_w)

    rows_v[...] = jnp.zeros_like(rows_v)
    rows_u[...] = jnp.zeros_like(rows_u)
    rows_w[...] = jnp.zeros_like(rows_w)
    far_b[wide] = jnp.zeros(far_b.shape[1:], far_b.dtype)
    far_r[wide] = jnp.zeros(far_r.shape[1:], far_r.dtype)

    for copy in copies_q:
        copy.wait_recv()
    total = send_q[0]
    for d in range(1, beads):
        total = total + recv_q[d]
    own_r[...] = total
    pos_out[...] = total

    @pl.when(has_high)
    def _():
        up_r.start()

    @pl.when(has_low)
    def _():
        down_r.start()

    def place(start, size, coords, weights):
        scaled = ROOT * coords
        norm = -0.5 * (scaled[0] * scaled[0] + scaled[1] * scaled[1] + scaled[2] * scaled[2])
        region = pl.ds(start, size)
        for x in range(3):
            rows_v[region, x, :] = scaled[x]
            rows_w[region, x, :] = scaled[x] * weights
        rows_v[region, 3, :] = norm
        rows_v[region, 4, :] = jnp.ones_like(norm)
        rows_w[region, 3, :] = weights
        return scaled, norm

    def features(start, size):
        for c in range(start, start + size, 8):
            group = pl.ds(c, 8)
            high, mid, low = split3(rows_v[group])
            far_b[group] = jnp.concatenate([high, high, mid, high, low, mid], axis=1).astype(
                jnp.bfloat16
            )
            value = rows_w[group]
            high = value.astype(jnp.bfloat16).astype(jnp.float32)
            far_r[group] = jnp.concatenate([high, value - high], axis=1).astype(jnp.bfloat16)

    scaled, norm = place(HALO, cells, total, own_w[...])
    for x in range(3):
        rows_u[:, x, :] = scaled[x]
    rows_u[:, 3, :] = jnp.ones_like(norm)
    rows_u[:, 4, :] = norm
    features(HALO, cells)

    @pl.when(has_low)
    def _():
        up_w.wait_recv()
        up_r.wait_recv()

    @pl.when(has_high)
    def _():
        down_w.wait_recv()
        down_r.wait_recv()

    place(0, HALO, low_r[...], low_w[...])
    features(0, HALO)
    place(HALO + cells, HALO, high_r[...], high_w[...])
    features(HALO + cells, HALO)

    def one_cell(c, carry):
        own = rows_u[c]
        high, mid, low = split3(own)
        stacked = jnp.concatenate([high, mid, high, low, high, mid], axis=0)
        stacked = jnp.concatenate(
            [stacked, jnp.zeros((slots - stacked.shape[0], slots), jnp.float32)], axis=0
        )
        left = jnp.transpose(stacked)[:, :48].astype(jnp.bfloat16)
        partners = [c + HALO]
        for n in range(neigh):
            entry = list_ref[c, n]
            local = jnp.clip(entry - space * cells + HALO, 0, wide - 1)
            partners.append(jnp.where(entry >= 0, local, wide))
        if len(partners) % 2:
            partners.append(wide)
        acc = jnp.zeros((16, slots), jnp.float32)
        for n in range(0, len(partners), 2):
            one, two = partners[n], partners[n + 1]
            right = jnp.concatenate([far_b[one], far_b[two]], axis=1)
            power = lax.dot_general(
                left, right, (((1,), (0,)), ((), ())), preferred_element_type=jnp.float32
            )
            value = jnp.exp2(power)
            near = value.astype(jnp.bfloat16)
            rest = (value - near.astype(jnp.float32)).astype(jnp.bfloat16)
            pulls = jnp.concatenate([far_r[one], far_r[two]], axis=1)
            contract = (((1,), (1,)), ((), ()))
            acc = acc + lax.dot_general(pulls, near, contract, preferred_element_type=jnp.float32)
            acc = acc + lax.dot_general(pulls, rest, contract, preferred_element_type=jnp.float32)
        sums = acc[0:8] + acc[8:16]
        weight = rows_w[c + HALO][3:4]
        rows_f[c] = (PAIR_SCALE / ROOT) * weight * (own * sums[3:4] - sums)
        return carry

    lax.fori_loop(0, cells, one_cell, 0)

    for copy in copies_p:
        copy.wait_recv()
    moved = send_p[0]
    for d in range(1, beads):
        moved = moved + recv_p[d]
    for x in range(3):
        force = rows_f[:, x, :]
        frc_out[x] = force
        mom_out[x] = moved[x] + 0.25 * force

    for copy in copies_q + copies_p:
        copy.wait_send()

    @pl.when(has_high)
    def _():
        up_w.wait_send()
        up_r.wait_send()

    @pl.when(has_low)
    def _():
        down_w.wait_send()
        down_r.wait_send()


def per_device(positions, momenta, forces, noise, masses, strengths, cell_counts, neighbour_cells):
    beads = lax.axis_size("bead")
    spaces = lax.axis_size("space")
    cells, slots = masses.shape
    wide = cells + 2 * HALO
    coef, kicks = propagator(beads)
    block = (3, cells, slots)
    f32 = jnp.float32
    vmem = pl.BlockSpec(memory_space=pltpu.VMEM)
    smem = pl.BlockSpec(memory_space=pltpu.SMEM)
    out = pl.pallas_call(
        functools.partial(kernel, beads, spaces, coef),
        out_shape=[jax.ShapeDtypeStruct(block, f32)] * 3,
        in_specs=[smem] * 3 + [vmem] * 6,
        out_specs=[vmem] * 3,
        scratch_shapes=[
            pltpu.VMEM((beads,) + block, f32),
            pltpu.VMEM((beads,) + block, f32),
            pltpu.VMEM((beads,) + block, f32),
            pltpu.VMEM((beads,) + block, f32),
            pltpu.VMEM(block, f32),
            pltpu.VMEM((cells, slots), f32),
            pltpu.VMEM((3, HALO, slots), f32),
            pltpu.VMEM((HALO, slots), f32),
            pltpu.VMEM((3, HALO, slots), f32),
            pltpu.VMEM((HALO, slots), f32),
            pltpu.VMEM((wide, 8, slots), f32),
            pltpu.VMEM((cells, 8, slots), f32),
            pltpu.VMEM((wide, 8, slots), f32),
            pltpu.VMEM((wide + 1, 48, slots), jnp.bfloat16),
            pltpu.VMEM((wide + 1, 16, slots), jnp.bfloat16),
            pltpu.VMEM((cells, 8, slots), f32),
            pltpu.SemaphoreType.DMA((beads,)),
            pltpu.SemaphoreType.DMA((beads,)),
            pltpu.SemaphoreType.DMA((beads,)),
            pltpu.SemaphoreType.DMA((beads,)),
            pltpu.SemaphoreType.DMA((4,)),
            pltpu.SemaphoreType.DMA((4,)),
        ],
        compiler_params=pltpu.CompilerParams(
            collective_id=0, has_side_effects=True, vmem_limit_bytes=32 * 1024 * 1024
        ),
    )(
        jnp.asarray(kicks),
        cell_counts,
        neighbour_cells,
        positions[0],
        momenta[0],
        forces[0],
        noise[0],
        masses,
        strengths,
    )
    return tuple(x[None] for x in out)


def solution(mesh):
    whole = P(("groups", "bead"), None, "space", None)
    in_specs = (
        whole,
        whole,
        whole,
        whole,
        P(("groups", "space"), None),
        P(("groups", "space"), None),
        P("groups"),
        P(("groups", "space"), None),
    )
    return jax.shard_map(
        per_device, mesh=mesh, in_specs=in_specs, out_specs=(whole,) * 3, check_vma=False
    )
```

```python
import functools
import math

import jax
import jax.numpy as jnp
import numpy as np
from jax import lax
from jax.experimental import pallas as pl
from jax.experimental.pallas import tpu as pltpu
from jax.sharding import PartitionSpec as P

HALO = 16
TIME_STEP = 0.5
CYCLE_FREQ = 1.5
GAMMA_ZERO = 0.5
PAIR_SCALE = 0.005
ROOT = math.sqrt(math.log2(math.e))
MESH = pl.DeviceIdType.MESH


def modes_table(beads):
    k = np.arange(beads)[:, None]
    j = np.arange(beads)[None, :]
    angle = 2.0 * np.pi * (k * j % beads) / beads
    parity = np.where(j % 2 == 0, 1.0, -1.0)
    plain = np.ones_like(angle) / np.sqrt(beads)
    factor = np.sqrt(2.0 / beads)
    return np.where(
        k == 0,
        plain,
        np.where(
            k < beads // 2,
            factor * np.cos(angle),
            np.where(k == beads // 2, parity * plain, factor * np.sin(angle)),
        ),
    )


def propagator(beads):
    table = modes_table(beads)
    k = np.arange(beads)
    freq = 2.0 * CYCLE_FREQ * np.sin(np.pi * k / beads)
    half = 0.5 * TIME_STEP
    cos, sin = np.cos(freq * half), np.sin(freq * half)
    reach = np.where(k == 0, half, sin / np.where(k == 0, 1.0, freq))
    damp = np.exp(-np.where(k == 0, GAMMA_ZERO, 2.0 * freq) * TIME_STEP)
    kick = np.sqrt(1.0 - damp * damp)
    pull = -freq * sin
    modes = {
        "qq": cos * cos + reach * damp * pull,
        "qp": reach * cos * (1.0 + damp),
        "pq": pull * cos * (1.0 + damp),
        "pp": pull * reach + cos * cos * damp,
    }
    by_offset = {
        name: [float(np.sum(value * table[:, 0] * table[:, d])) for d in range(beads)]
        for name, value in modes.items()
    }
    noise = np.stack([(reach * kick)[:, None] * table, (cos * kick)[:, None] * table])
    return by_offset, noise.astype(np.float32)


def split3(value):
    high = value.astype(jnp.bfloat16).astype(jnp.float32)
    rest = value - high
    mid = rest.astype(jnp.bfloat16).astype(jnp.float32)
    return high, mid, rest - mid


def kernel(
    beads,
    spaces,
    coef,
    kicks_ref,
    counts_ref,
    list_ref,
    pos_ref,
    mom_ref,
    frc_ref,
    noi_ref,
    mass_ref,
    str_ref,
    pos_out,
    mom_out,
    frc_out,
    send_q,
    send_p,
    recv_q,
    recv_p,
    own_r,
    own_w,
    low_r,
    low_w,
    high_r,
    high_w,
    rows_v,
    rows_u,
    rows_w,
    far_b,
    far_r,
    rows_f,
    sq_sem,
    rq_sem,
    sp_sem,
    rp_sem,
    halo_send,
    halo_recv,
):
    bead = lax.axis_index("bead")
    space = lax.axis_index("space")
    cells, slots = mass_ref.shape
    neigh = list_ref.shape[1]
    wide = cells + 2 * HALO
    has_low = space > 0
    has_high = space < spaces - 1

    barrier = pltpu.get_barrier_semaphore()
    for d in range(1, beads):
        pl.semaphore_signal(
            barrier, inc=1, device_id={"bead": lax.rem(bead + d, beads)}, device_id_type=MESH
        )

    @pl.when(has_low)
    def _():
        pl.semaphore_signal(barrier, inc=1, device_id={"space": space - 1}, device_id_type=MESH)

    @pl.when(has_high)
    def _():
        pl.semaphore_signal(barrier, inc=1, device_id={"space": space + 1}, device_id_type=MESH)

    mass = mass_ref[...][None]
    root_mass = jnp.sqrt(mass)
    q = pos_ref[...]
    p = mom_ref[...] + 0.25 * frc_ref[...]
    scaled_p = p / mass
    noise_q = noi_ref[...] / root_mass
    for d in range(beads):
        target = lax.rem(bead + d, beads)
        send_q[d] = coef["qq"][d] * q + coef["qp"][d] * scaled_p + kicks_ref[0, bead, target] * noise_q

    lane = lax.broadcasted_iota(jnp.int32, (1, slots), 1)
    for c in range(cells):
        count = counts_ref[space * cells + c]
        own_w[c : c + 1, :] = jnp.where(lane < count, str_ref[c : c + 1, :], 0.0)

    pl.semaphore_wait(
        barrier, beads - 1 + has_low.astype(jnp.int32) + has_high.astype(jnp.int32)
    )

    def bead_copy(source, target, send, recv, d):
        return pltpu.make_async_remote_copy(
            src_ref=source.at[d],
            dst_ref=target.at[d],
            send_sem=send.at[d],
            recv_sem=recv.at[d],
            device_id={"bead": lax.rem(bead + d, beads)},
            device_id_type=MESH,
        )

    def space_copy(source, target, index, peer):
        return pltpu.make_async_remote_copy(
            src_ref=source,
            dst_ref=target,
            send_sem=halo_send.at[index],
            recv_sem=halo_recv.at[index],
            device_id={"space": peer},
            device_id_type=MESH,
        )

    first = pl.ds(0, HALO)
    last = pl.ds(cells - HALO, HALO)
    up_w = space_copy(own_w.at[last], low_w, 0, space + 1)
    down_w = space_copy(own_w.at[first], high_w, 1, space - 1)
    up_r = space_copy(own_r.at[:, last], low_r, 2, space + 1)
    down_r = space_copy(own_r.at[:, first], high_r, 3, space - 1)
    copies_q = [bead_copy(send_q, recv_q, sq_sem, rq_sem, d) for d in range(1, beads)]
    copies_p = [bead_copy(send_p, recv_p, sp_sem, rp_sem, d) for d in range(1, beads)]
    for copy in copies_q:
        copy.start()

    @pl.when(has_high)
    def _():
        up_w.start()

    @pl.when(has_low)
    def _():
        down_w.start()

    mass_q = mass * q
    noise_p = noi_ref[...] * root_mass
    for d in range(beads):
        target = lax.rem(bead + d, beads)
        send_p[d] = coef["pq"][d] * mass_q + coef["pp"][d] * p + kicks_ref[1, bead, target] * noise_p
    for copy in copies_p:
        copy.start()

    @pl.when(jnp.logical_not(has_low))
    def _():
        low_r[...] = jnp.zeros_like(low_r)
        low_w[...] = jnp.zeros_like(low_w)

    @pl.when(jnp.logical_not(has_high))
    def _():
        high_r[...] = jnp.zeros_like(high_r)
        high_w[...] = jnp.zeros_like(high_w)

    rows_v[...] = jnp.zeros_like(rows_v)
    rows_u[...] = jnp.zeros_like(rows_u)
    rows_w[...] = jnp.zeros_like(rows_w)
    far_b[wide] = jnp.zeros(far_b.shape[1:], far_b.dtype)
    far_r[wide] = jnp.zeros(far_r.shape[1:], far_r.dtype)

    for copy in copies_q:
        copy.wait_recv()
    total = send_q[0]
    for d in range(1, beads):
        total = total + recv_q[d]
    own_r[...] = total
    pos_out[...] = total

    @pl.when(has_high)
    def _():
        up_r.start()

    @pl.when(has_low)
    def _():
        down_r.start()

    def place(start, size, coords, weights):
        scaled = ROOT * coords
        norm = -0.5 * (scaled[0] * scaled[0] + scaled[1] * scaled[1] + scaled[2] * scaled[2])
        region = pl.ds(start, size)
        for x in range(3):
            rows_v[region, x, :] = scaled[x]
            rows_w[region, x, :] = scaled[x] * weights
        rows_v[region, 3, :] = norm
        rows_v[region, 4, :] = jnp.ones_like(norm)
        rows_w[region, 3, :] = weights
        return scaled, norm

    def features(start, size):
        pad = jnp.zeros((slots - 48, slots), jnp.float32)

        def group_of(g, carry):
            group = pl.ds(pl.multiple_of(start + g * 8, 8), 8)
            high, mid, low = split3(rows_v[group])
            stacked = jnp.concatenate([high, high, mid, high, low, mid], axis=1)
            value = rows_w[group]
            near = value.astype(jnp.bfloat16).astype(jnp.float32)
            far_r[group] = jnp.concatenate([near, value - near], axis=1).astype(jnp.bfloat16)
            for i in range(8):
                turned = jnp.transpose(jnp.concatenate([stacked[i], pad], axis=0))
                far_b[start + g * 8 + i] = turned.astype(jnp.bfloat16)
            return carry

        lax.fori_loop(0, size // 8, group_of, 0)

    scaled, norm = place(HALO, cells, total, own_w[...])
    for x in range(3):
        rows_u[:, x, :] = scaled[x]
    rows_u[:, 3, :] = jnp.ones_like(norm)
    rows_u[:, 4, :] = norm
    features(HALO, cells)

    @pl.when(has_low)
    def _():
        up_w.wait_recv()
        up_r.wait_recv()

    @pl.when(has_high)
    def _():
        down_w.wait_recv()
        down_r.wait_recv()

    place(0, HALO, low_r[...], low_w[...])
    features(0, HALO)
    place(HALO + cells, HALO, high_r[...], high_w[...])
    features(HALO + cells, HALO)

    def one_cell(c, carry):
        own = rows_u[c]
        high, mid, low = split3(own)
        right = jnp.concatenate([high, mid, high, low, high, mid], axis=0).astype(jnp.bfloat16)
        partners = [c + HALO]
        for n in range(neigh):
            entry = list_ref[c, n]
            local = jnp.clip(entry - space * cells + HALO, 0, wide - 1)
            partners.append(jnp.where(entry >= 0, local, wide))
        if len(partners) % 2:
            partners.append(wide)
        acc = jnp.zeros((16, 2 * slots), jnp.float32)
        contract = (((1,), (0,)), ((), ()))
        for n in range(0, len(partners), 2):
            one, two = partners[n], partners[n + 1]
            left = jnp.concatenate([far_b[one][:, :48], far_b[two][:, :48]], axis=0)
            power = lax.dot_general(left, right, contract, preferred_element_type=jnp.float32)
            value = jnp.exp2(power)
            near = value.astype(jnp.bfloat16)
            rest = (value - near.astype(jnp.float32)).astype(jnp.bfloat16)
            acc = acc + lax.dot_general(
                jnp.concatenate([far_r[one], far_r[two]], axis=1),
                jnp.concatenate([near, rest], axis=1),
                contract,
                preferred_element_type=jnp.float32,
            )
        acc = acc[:, :slots] + acc[:, slots:]
        sums = acc[0:8] + acc[8:16]
        weight = rows_w[c + HALO][3:4]
        rows_f[c] = (PAIR_SCALE / ROOT) * weight * (own * sums[3:4] - sums)
        return carry

    lax.fori_loop(0, cells, one_cell, 0)

    for copy in copies_p:
        copy.wait_recv()
    moved = send_p[0]
    for d in range(1, beads):
        moved = moved + recv_p[d]
    for x in range(3):
        force = rows_f[:, x, :]
        frc_out[x] = force
        mom_out[x] = moved[x] + 0.25 * force

    for copy in copies_q + copies_p:
        copy.wait_send()

    @pl.when(has_high)
    def _():
        up_w.wait_send()
        up_r.wait_send()

    @pl.when(has_low)
    def _():
        down_w.wait_send()
        down_r.wait_send()


def per_device(positions, momenta, forces, noise, masses, strengths, cell_counts, neighbour_cells):
    beads = lax.axis_size("bead")
    spaces = lax.axis_size("space")
    cells, slots = masses.shape
    wide = cells + 2 * HALO
    coef, kicks = propagator(beads)
    block = (3, cells, slots)
    f32 = jnp.float32
    vmem = pl.BlockSpec(memory_space=pltpu.VMEM)
    smem = pl.BlockSpec(memory_space=pltpu.SMEM)
    out = pl.pallas_call(
        functools.partial(kernel, beads, spaces, coef),
        out_shape=[jax.ShapeDtypeStruct(block, f32)] * 3,
        in_specs=[smem] * 3 + [vmem] * 6,
        out_specs=[vmem] * 3,
        scratch_shapes=[
            pltpu.VMEM((beads,) + block, f32),
            pltpu.VMEM((beads,) + block, f32),
            pltpu.VMEM((beads,) + block, f32),
            pltpu.VMEM((beads,) + block, f32),
            pltpu.VMEM(block, f32),
            pltpu.VMEM((cells, slots), f32),
            pltpu.VMEM((3, HALO, slots), f32),
            pltpu.VMEM((HALO, slots), f32),
            pltpu.VMEM((3, HALO, slots), f32),
            pltpu.VMEM((HALO, slots), f32),
            pltpu.VMEM((wide, 8, slots), f32),
            pltpu.VMEM((cells, 8, slots), f32),
            pltpu.VMEM((wide, 8, slots), f32),
            pltpu.VMEM((wide + 1, slots, slots), jnp.bfloat16),
            pltpu.VMEM((wide + 1, 16, slots), jnp.bfloat16),
            pltpu.VMEM((cells, 8, slots), f32),
            pltpu.SemaphoreType.DMA((beads,)),
            pltpu.SemaphoreType.DMA((beads,)),
            pltpu.SemaphoreType.DMA((beads,)),
            pltpu.SemaphoreType.DMA((beads,)),
            pltpu.SemaphoreType.DMA((4,)),
            pltpu.SemaphoreType.DMA((4,)),
        ],
        compiler_params=pltpu.CompilerParams(
            collective_id=0, has_side_effects=True, vmem_limit_bytes=32 * 1024 * 1024
        ),
    )(
        jnp.asarray(kicks),
        cell_counts,
        neighbour_cells,
        positions[0],
        momenta[0],
        forces[0],
        noise[0],
        masses,
        strengths,
    )
    return tuple(x[None] for x in out)


def solution(mesh):
    whole = P(("groups", "bead"), None, "space", None)
    in_specs = (
        whole,
        whole,
        whole,
        whole,
        P(("groups", "space"), None),
        P(("groups", "space"), None),
        P("groups"),
        P(("groups", "space"), None),
    )
    return jax.shard_map(
        per_device, mesh=mesh, in_specs=in_specs, out_specs=(whole,) * 3, check_vma=False
    )
```

```python
import functools
import math

import jax
import jax.numpy as jnp
import numpy as np
from jax import lax
from jax.experimental import pallas as pl
from jax.experimental.pallas import tpu as pltpu
from jax.sharding import PartitionSpec as P

HALO = 16
TIME_STEP = 0.5
CYCLE_FREQ = 1.5
GAMMA_ZERO = 0.5
PAIR_SCALE = 0.005
ROOT = math.sqrt(math.log2(math.e))
MESH = pl.DeviceIdType.MESH


def modes_table(beads):
    k = np.arange(beads)[:, None]
    j = np.arange(beads)[None, :]
    angle = 2.0 * np.pi * (k * j % beads) / beads
    parity = np.where(j % 2 == 0, 1.0, -1.0)
    plain = np.ones_like(angle) / np.sqrt(beads)
    factor = np.sqrt(2.0 / beads)
    return np.where(
        k == 0,
        plain,
        np.where(
            k < beads // 2,
            factor * np.cos(angle),
            np.where(k == beads // 2, parity * plain, factor * np.sin(angle)),
        ),
    )


def propagator(beads):
    table = modes_table(beads)
    k = np.arange(beads)
    freq = 2.0 * CYCLE_FREQ * np.sin(np.pi * k / beads)
    half = 0.5 * TIME_STEP
    cos, sin = np.cos(freq * half), np.sin(freq * half)
    reach = np.where(k == 0, half, sin / np.where(k == 0, 1.0, freq))
    damp = np.exp(-np.where(k == 0, GAMMA_ZERO, 2.0 * freq) * TIME_STEP)
    kick = np.sqrt(1.0 - damp * damp)
    pull = -freq * sin
    modes = {
        "qq": cos * cos + reach * damp * pull,
        "qp": reach * cos * (1.0 + damp),
        "pq": pull * cos * (1.0 + damp),
        "pp": pull * reach + cos * cos * damp,
    }
    by_offset = {
        name: [float(np.sum(value * table[:, 0] * table[:, d])) for d in range(beads)]
        for name, value in modes.items()
    }
    noise = np.stack([(reach * kick)[:, None] * table, (cos * kick)[:, None] * table])
    return by_offset, noise.astype(np.float32)


def split3(value):
    high = value.astype(jnp.bfloat16).astype(jnp.float32)
    rest = value - high
    mid = rest.astype(jnp.bfloat16).astype(jnp.float32)
    return high, mid, rest - mid


def kernel(
    beads,
    spaces,
    coef,
    kicks_ref,
    counts_ref,
    list_ref,
    pos_ref,
    mom_ref,
    frc_ref,
    noi_ref,
    mass_ref,
    str_ref,
    pos_out,
    mom_out,
    frc_out,
    send_q,
    send_p,
    recv_q,
    recv_p,
    own_r,
    own_w,
    low_r,
    low_w,
    high_r,
    high_w,
    rows_v,
    rows_u,
    rows_w,
    far_b,
    far_r,
    rows_f,
    listed,
    sq_sem,
    rq_sem,
    sp_sem,
    rp_sem,
    halo_send,
    halo_recv,
):
    bead = lax.axis_index("bead")
    space = lax.axis_index("space")
    cells, slots = mass_ref.shape
    neigh = list_ref.shape[1]
    wide = cells + 2 * HALO
    has_low = space > 0
    has_high = space < spaces - 1

    barrier = pltpu.get_barrier_semaphore()
    for d in range(1, beads):
        pl.semaphore_signal(
            barrier, inc=1, device_id={"bead": lax.rem(bead + d, beads)}, device_id_type=MESH
        )

    @pl.when(has_low)
    def _():
        pl.semaphore_signal(barrier, inc=1, device_id={"space": space - 1}, device_id_type=MESH)

    @pl.when(has_high)
    def _():
        pl.semaphore_signal(barrier, inc=1, device_id={"space": space + 1}, device_id_type=MESH)

    mass = mass_ref[...][None]
    root_mass = jnp.sqrt(mass)
    q = pos_ref[...]
    p = mom_ref[...] + 0.25 * frc_ref[...]
    scaled_p = p / mass
    noise_q = noi_ref[...] / root_mass
    for d in range(beads):
        target = lax.rem(bead + d, beads)
        send_q[d] = coef["qq"][d] * q + coef["qp"][d] * scaled_p + kicks_ref[0, bead, target] * noise_q

    lane = lax.broadcasted_iota(jnp.int32, (1, slots), 1)
    for c in range(cells):
        count = counts_ref[space * cells + c]
        own_w[c : c + 1, :] = jnp.where(lane < count, str_ref[c : c + 1, :], 0.0)

    pl.semaphore_wait(
        barrier, beads - 1 + has_low.astype(jnp.int32) + has_high.astype(jnp.int32)
    )

    def bead_copy(source, target, send, recv, d):
        return pltpu.make_async_remote_copy(
            src_ref=source.at[d],
            dst_ref=target.at[d],
            send_sem=send.at[d],
            recv_sem=recv.at[d],
            device_id={"bead": lax.rem(bead + d, beads)},
            device_id_type=MESH,
        )

    def space_copy(source, target, index, peer):
        return pltpu.make_async_remote_copy(
            src_ref=source,
            dst_ref=target,
            send_sem=halo_send.at[index],
            recv_sem=halo_recv.at[index],
            device_id={"space": peer},
            device_id_type=MESH,
        )

    first = pl.ds(0, HALO)
    last = pl.ds(cells - HALO, HALO)
    up_w = space_copy(own_w.at[last], low_w, 0, space + 1)
    down_w = space_copy(own_w.at[first], high_w, 1, space - 1)
    up_r = space_copy(own_r.at[:, last], low_r, 2, space + 1)
    down_r = space_copy(own_r.at[:, first], high_r, 3, space - 1)
    copies_q = [bead_copy(send_q, recv_q, sq_sem, rq_sem, d) for d in range(1, beads)]
    copies_p = [bead_copy(send_p, recv_p, sp_sem, rp_sem, d) for d in range(1, beads)]
    for copy in copies_q:
        copy.start()

    @pl.when(has_high)
    def _():
        up_w.start()

    @pl.when(has_low)
    def _():
        down_w.start()

    mass_q = mass * q
    noise_p = noi_ref[...] * root_mass
    for d in range(beads):
        target = lax.rem(bead + d, beads)
        send_p[d] = coef["pq"][d] * mass_q + coef["pp"][d] * p + kicks_ref[1, bead, target] * noise_p
    for copy in copies_p:
        copy.start()

    @pl.when(jnp.logical_not(has_low))
    def _():
        low_r[...] = jnp.zeros_like(low_r)
        low_w[...] = jnp.zeros_like(low_w)

    @pl.when(jnp.logical_not(has_high))
    def _():
        high_r[...] = jnp.zeros_like(high_r)
        high_w[...] = jnp.zeros_like(high_w)

    rows_v[...] = jnp.zeros_like(rows_v)
    rows_u[...] = jnp.zeros_like(rows_u)
    rows_w[...] = jnp.zeros_like(rows_w)
    entries = list_ref[...]
    row = lax.broadcasted_iota(jnp.int32, (cells, 1), 0) + space * cells
    shifted = jnp.where(entries >= 0, entries - row + HALO + 1, -1)
    column = lax.broadcasted_iota(jnp.int32, (cells, slots), 1)
    found = column == HALO + 1
    for n in range(neigh):
        found = jnp.logical_or(found, shifted[:, n : n + 1] == column)
    listed[...] = jnp.where(found, 1.0, 0.0)

    for copy in copies_q:
        copy.wait_recv()
    total = send_q[0]
    for d in range(1, beads):
        total = total + recv_q[d]
    own_r[...] = total
    pos_out[...] = total

    @pl.when(has_high)
    def _():
        up_r.start()

    @pl.when(has_low)
    def _():
        down_r.start()

    def place(start, size, coords, weights):
        scaled = ROOT * coords
        norm = -0.5 * (scaled[0] * scaled[0] + scaled[1] * scaled[1] + scaled[2] * scaled[2])
        region = pl.ds(start, size)
        for x in range(3):
            rows_v[region, x, :] = scaled[x]
            rows_w[region, x, :] = scaled[x] * weights
        rows_v[region, 3, :] = norm
        rows_v[region, 4, :] = jnp.ones_like(norm)
        rows_w[region, 3, :] = weights
        return scaled, norm

    def features(start, size):
        pad = jnp.zeros((slots - 48, slots), jnp.float32)

        def group_of(g, carry):
            group = pl.ds(pl.multiple_of(start + g * 8, 8), 8)
            high, mid, low = split3(rows_v[group])
            stacked = jnp.concatenate([high, high, mid, high, low, mid], axis=1)
            value = rows_w[group]
            near = value.astype(jnp.bfloat16).astype(jnp.float32)
            far_r[group] = jnp.concatenate([near, value - near], axis=1).astype(jnp.bfloat16)
            for i in range(8):
                turned = jnp.transpose(jnp.concatenate([stacked[i], pad], axis=0))
                far_b[start + g * 8 + i] = turned.astype(jnp.bfloat16)
            return carry

        lax.fori_loop(0, size // 8, group_of, 0)

    scaled, norm = place(HALO, cells, total, own_w[...])
    for x in range(3):
        rows_u[:, x, :] = scaled[x]
    rows_u[:, 3, :] = jnp.ones_like(norm)
    rows_u[:, 4, :] = norm
    features(HALO, cells)

    @pl.when(has_low)
    def _():
        up_w.wait_recv()
        up_r.wait_recv()

    @pl.when(has_high)
    def _():
        down_w.wait_recv()
        down_r.wait_recv()

    place(0, HALO, low_r[...], low_w[...])
    features(0, HALO)
    place(HALO + cells, HALO, high_r[...], high_w[...])
    features(HALO + cells, HALO)

    def own_part(c):
        high, mid, low = split3(rows_u[c])
        return jnp.concatenate([high, mid, high, low, high, mid], axis=0).astype(jnp.bfloat16)

    contract = (((1,), (0,)), ((), ()))

    def one_pair(pair, carry):
        c = 2 * pair
        right = jnp.concatenate([own_part(c), own_part(c + 1)], axis=1)
        flags = listed[pl.ds(c, 1), :], listed[pl.ds(c + 1, 1), :]

        def pulls(t, which):
            flag = flags[which][:, t + 1 - which : t + 2 - which]
            return far_r[c + t] * jnp.broadcast_to(flag, (16, slots)).astype(jnp.bfloat16)

        acc = jnp.zeros((32, 4 * slots), jnp.float32)
        for t in range(0, 2 * HALO + 2, 2):
            left = jnp.concatenate([far_b[c + t][:, :48], far_b[c + t + 1][:, :48]], axis=0)
            power = lax.dot_general(left, right, contract, preferred_element_type=jnp.float32)
            value = jnp.exp2(power)
            near = value.astype(jnp.bfloat16)
            rest = (value - near.astype(jnp.float32)).astype(jnp.bfloat16)
            sides = [
                jnp.concatenate([pulls(t + i, which) for which in range(2)], axis=0)
                for i in range(2)
            ]
            acc = acc + lax.dot_general(
                jnp.concatenate(sides, axis=1),
                jnp.concatenate([near, rest], axis=1),
                contract,
                preferred_element_type=jnp.float32,
            )
        acc = acc[:, : 2 * slots] + acc[:, 2 * slots :]
        for which in range(2):
            part = acc[16 * which : 16 * which + 16, which * slots : (which + 1) * slots]
            sums = part[0:8] + part[8:16]
            own = rows_u[c + which]
            weight = rows_w[c + which + HALO][3:4]
            rows_f[c + which] = (PAIR_SCALE / ROOT) * weight * (own * sums[3:4] - sums)
        return carry

    lax.fori_loop(0, cells // 2, one_pair, 0)

    for copy in copies_p:
        copy.wait_recv()
    moved = send_p[0]
    for d in range(1, beads):
        moved = moved + recv_p[d]
    for x in range(3):
        force = rows_f[:, x, :]
        frc_out[x] = force
        mom_out[x] = moved[x] + 0.25 * force

    for copy in copies_q + copies_p:
        copy.wait_send()

    @pl.when(has_high)
    def _():
        up_w.wait_send()
        up_r.wait_send()

    @pl.when(has_low)
    def _():
        down_w.wait_send()
        down_r.wait_send()


def per_device(positions, momenta, forces, noise, masses, strengths, cell_counts, neighbour_cells):
    beads = lax.axis_size("bead")
    spaces = lax.axis_size("space")
    cells, slots = masses.shape
    wide = cells + 2 * HALO
    coef, kicks = propagator(beads)
    block = (3, cells, slots)
    f32 = jnp.float32
    vmem = pl.BlockSpec(memory_space=pltpu.VMEM)
    smem = pl.BlockSpec(memory_space=pltpu.SMEM)
    out = pl.pallas_call(
        functools.partial(kernel, beads, spaces, coef),
        out_shape=[jax.ShapeDtypeStruct(block, f32)] * 3,
        in_specs=[smem] * 2 + [vmem] * 7,
        out_specs=[vmem] * 3,
        scratch_shapes=[
            pltpu.VMEM((beads,) + block, f32),
            pltpu.VMEM((beads,) + block, f32),
            pltpu.VMEM((beads,) + block, f32),
            pltpu.VMEM((beads,) + block, f32),
            pltpu.VMEM(block, f32),
            pltpu.VMEM((cells, slots), f32),
            pltpu.VMEM((3, HALO, slots), f32),
            pltpu.VMEM((HALO, slots), f32),
            pltpu.VMEM((3, HALO, slots), f32),
            pltpu.VMEM((HALO, slots), f32),
            pltpu.VMEM((wide, 8, slots), f32),
            pltpu.VMEM((cells, 8, slots), f32),
            pltpu.VMEM((wide, 8, slots), f32),
            pltpu.VMEM((wide, slots, slots), jnp.bfloat16),
            pltpu.VMEM((wide, 16, slots), jnp.bfloat16),
            pltpu.VMEM((cells, 8, slots), f32),
            pltpu.VMEM((cells, slots), f32),
            pltpu.SemaphoreType.DMA((beads,)),
            pltpu.SemaphoreType.DMA((beads,)),
            pltpu.SemaphoreType.DMA((beads,)),
            pltpu.SemaphoreType.DMA((beads,)),
            pltpu.SemaphoreType.DMA((4,)),
            pltpu.SemaphoreType.DMA((4,)),
        ],
        compiler_params=pltpu.CompilerParams(
            collective_id=0, has_side_effects=True, vmem_limit_bytes=32 * 1024 * 1024
        ),
    )(
        jnp.asarray(kicks),
        cell_counts,
        neighbour_cells,
        positions[0],
        momenta[0],
        forces[0],
        noise[0],
        masses,
        strengths,
    )
    return tuple(x[None] for x in out)


def solution(mesh):
    whole = P(("groups", "bead"), None, "space", None)
    in_specs = (
        whole,
        whole,
        whole,
        whole,
        P(("groups", "space"), None),
        P(("groups", "space"), None),
        P("groups"),
        P(("groups", "space"), None),
    )
    return jax.shard_map(
        per_device, mesh=mesh, in_specs=in_specs, out_specs=(whole,) * 3, check_vma=False
    )
```

```python
import functools
import math

import jax
import jax.numpy as jnp
import numpy as np
from jax import lax
from jax.experimental import pallas as pl
from jax.experimental.pallas import tpu as pltpu
from jax.sharding import PartitionSpec as P

HALO = 16
TIME_STEP = 0.5
CYCLE_FREQ = 1.5
GAMMA_ZERO = 0.5
PAIR_SCALE = 0.005
ROOT = math.sqrt(math.log2(math.e))
MESH = pl.DeviceIdType.MESH


def modes_table(beads):
    k = np.arange(beads)[:, None]
    j = np.arange(beads)[None, :]
    angle = 2.0 * np.pi * (k * j % beads) / beads
    parity = np.where(j % 2 == 0, 1.0, -1.0)
    plain = np.ones_like(angle) / np.sqrt(beads)
    factor = np.sqrt(2.0 / beads)
    return np.where(
        k == 0,
        plain,
        np.where(
            k < beads // 2,
            factor * np.cos(angle),
            np.where(k == beads // 2, parity * plain, factor * np.sin(angle)),
        ),
    )


def propagator(beads):
    table = modes_table(beads)
    k = np.arange(beads)
    freq = 2.0 * CYCLE_FREQ * np.sin(np.pi * k / beads)
    half = 0.5 * TIME_STEP
    cos, sin = np.cos(freq * half), np.sin(freq * half)
    reach = np.where(k == 0, half, sin / np.where(k == 0, 1.0, freq))
    damp = np.exp(-np.where(k == 0, GAMMA_ZERO, 2.0 * freq) * TIME_STEP)
    kick = np.sqrt(1.0 - damp * damp)
    pull = -freq * sin
    modes = {
        "qq": cos * cos + reach * damp * pull,
        "qp": reach * cos * (1.0 + damp),
        "pq": pull * cos * (1.0 + damp),
        "pp": pull * reach + cos * cos * damp,
    }
    by_offset = {
        name: [float(np.sum(value * table[:, 0] * table[:, d])) for d in range(beads)]
        for name, value in modes.items()
    }
    noise = np.stack([(reach * kick)[:, None] * table, (cos * kick)[:, None] * table])
    return by_offset, noise.astype(np.float32)


def split3(value):
    high = value.astype(jnp.bfloat16).astype(jnp.float32)
    rest = value - high
    mid = rest.astype(jnp.bfloat16).astype(jnp.float32)
    return high, mid, rest - mid


def kernel(
    beads,
    spaces,
    coef,
    kicks_ref,
    counts_ref,
    list_ref,
    pos_ref,
    mom_ref,
    frc_ref,
    noi_ref,
    mass_ref,
    str_ref,
    pos_out,
    mom_out,
    frc_out,
    send_q,
    send_p,
    recv_q,
    recv_p,
    own_r,
    own_w,
    low_r,
    low_w,
    high_r,
    high_w,
    rows_v,
    rows_u,
    rows_w,
    far_b,
    far_r,
    rows_f,
    sq_sem,
    rq_sem,
    sp_sem,
    rp_sem,
    halo_send,
    halo_recv,
):
    bead = lax.axis_index("bead")
    space = lax.axis_index("space")
    cells, slots = mass_ref.shape
    neigh = list_ref.shape[1]
    wide = cells + 2 * HALO
    has_low = space > 0
    has_high = space < spaces - 1

    barrier = pltpu.get_barrier_semaphore()
    for d in range(1, beads):
        pl.semaphore_signal(
            barrier, inc=1, device_id={"bead": lax.rem(bead + d, beads)}, device_id_type=MESH
        )

    @pl.when(has_low)
    def _():
        pl.semaphore_signal(barrier, inc=1, device_id={"space": space - 1}, device_id_type=MESH)

    @pl.when(has_high)
    def _():
        pl.semaphore_signal(barrier, inc=1, device_id={"space": space + 1}, device_id_type=MESH)

    mass = mass_ref[...][None]
    root_mass = jnp.sqrt(mass)
    q = pos_ref[...]
    p = mom_ref[...] + 0.25 * frc_ref[...]
    scaled_p = p / mass
    noise_q = noi_ref[...] / root_mass
    for d in range(beads):
        target = lax.rem(bead + d, beads)
        send_q[d] = coef["qq"][d] * q + coef["qp"][d] * scaled_p + kicks_ref[0, bead, target] * noise_q

    lane = lax.broadcasted_iota(jnp.int32, (1, slots), 1)
    for c in range(cells):
        count = counts_ref[space * cells + c]
        own_w[c : c + 1, :] = jnp.where(lane < count, str_ref[c : c + 1, :], 0.0)

    pl.semaphore_wait(
        barrier, beads - 1 + has_low.astype(jnp.int32) + has_high.astype(jnp.int32)
    )

    def bead_copy(source, target, send, recv, d):
        return pltpu.make_async_remote_copy(
            src_ref=source.at[d],
            dst_ref=target.at[d],
            send_sem=send.at[d],
            recv_sem=recv.at[d],
            device_id={"bead": lax.rem(bead + d, beads)},
            device_id_type=MESH,
        )

    def space_copy(source, target, index, peer):
        return pltpu.make_async_remote_copy(
            src_ref=source,
            dst_ref=target,
            send_sem=halo_send.at[index],
            recv_sem=halo_recv.at[index],
            device_id={"space": peer},
            device_id_type=MESH,
        )

    first = pl.ds(0, HALO)
    last = pl.ds(cells - HALO, HALO)
    up_w = space_copy(own_w.at[last], low_w, 0, space + 1)
    down_w = space_copy(own_w.at[first], high_w, 1, space - 1)
    up_r = space_copy(own_r.at[:, last], low_r, 2, space + 1)
    down_r = space_copy(own_r.at[:, first], high_r, 3, space - 1)
    copies_q = [bead_copy(send_q, recv_q, sq_sem, rq_sem, d) for d in range(1, beads)]
    copies_p = [bead_copy(send_p, recv_p, sp_sem, rp_sem, d) for d in range(1, beads)]
    for copy in copies_q:
        copy.start()

    @pl.when(has_high)
    def _():
        up_w.start()

    @pl.when(has_low)
    def _():
        down_w.start()

    mass_q = mass * q
    noise_p = noi_ref[...] * root_mass
    for d in range(beads):
        target = lax.rem(bead + d, beads)
        send_p[d] = coef["pq"][d] * mass_q + coef["pp"][d] * p + kicks_ref[1, bead, target] * noise_p
    for copy in copies_p:
        copy.start()

    @pl.when(jnp.logical_not(has_low))
    def _():
        low_r[...] = jnp.zeros_like(low_r)
        low_w[...] = jnp.zeros_like(low_w)

    @pl.when(jnp.logical_not(has_high))
    def _():
        high_r[...] = jnp.zeros_like(high_r)
        high_w[...] = jnp.zeros_like(high_w)

    rows_v[...] = jnp.zeros_like(rows_v)
    rows_u[...] = jnp.zeros_like(rows_u)
    rows_w[...] = jnp.zeros_like(rows_w)
    far_b[wide] = jnp.zeros(far_b.shape[1:], far_b.dtype)
    far_r[wide] = jnp.zeros(far_r.shape[1:], far_r.dtype)

    for copy in copies_q:
        copy.wait_recv()
    total = send_q[0]
    for d in range(1, beads):
        total = total + recv_q[d]
    own_r[...] = total
    pos_out[...] = total

    @pl.when(has_high)
    def _():
        up_r.start()

    @pl.when(has_low)
    def _():
        down_r.start()

    def place(start, size, coords, weights):
        scaled = ROOT * coords
        norm = -0.5 * (scaled[0] * scaled[0] + scaled[1] * scaled[1] + scaled[2] * scaled[2])
        region = pl.ds(start, size)
        for x in range(3):
            rows_v[region, x, :] = scaled[x]
            rows_w[region, x, :] = scaled[x] * weights
        rows_v[region, 3, :] = norm
        rows_v[region, 4, :] = jnp.ones_like(norm)
        rows_w[region, 3, :] = weights
        return scaled, norm

    def features(start, size):
        pad = jnp.zeros((slots - 48, slots), jnp.float32)

        def group_of(g, carry):
            group = pl.ds(pl.multiple_of(start + g * 8, 8), 8)
            high, mid, low = split3(rows_v[group])
            stacked = jnp.concatenate([high, high, mid, high, low, mid], axis=1)
            value = rows_w[group]
            near = value.astype(jnp.bfloat16).astype(jnp.float32)
            far_r[group] = jnp.concatenate([near, value - near], axis=1).astype(jnp.bfloat16)
            for i in range(8):
                turned = jnp.transpose(jnp.concatenate([stacked[i], pad], axis=0))
                far_b[start + g * 8 + i] = turned.astype(jnp.bfloat16)
            return carry

        lax.fori_loop(0, size // 8, group_of, 0, unroll=True)

    scaled, norm = place(HALO, cells, total, own_w[...])
    for x in range(3):
        rows_u[:, x, :] = scaled[x]
    rows_u[:, 3, :] = jnp.ones_like(norm)
    rows_u[:, 4, :] = norm
    features(HALO, cells)

    @pl.when(has_low)
    def _():
        up_w.wait_recv()
        up_r.wait_recv()

    @pl.when(has_high)
    def _():
        down_w.wait_recv()
        down_r.wait_recv()

    place(0, HALO, low_r[...], low_w[...])
    features(0, HALO)
    place(HALO + cells, HALO, high_r[...], high_w[...])
    features(HALO + cells, HALO)

    def one_cell(c, carry):
        own = rows_u[c]
        high, mid, low = split3(own)
        right = jnp.concatenate([high, mid, high, low, high, mid], axis=0).astype(jnp.bfloat16)
        partners = [c + HALO]
        for n in range(neigh):
            entry = list_ref[c, n]
            local = jnp.clip(entry - space * cells + HALO, 0, wide - 1)
            partners.append(jnp.where(entry >= 0, local, wide))
        if len(partners) % 2:
            partners.append(wide)
        acc = jnp.zeros((16, 2 * slots), jnp.float32)
        contract = (((1,), (0,)), ((), ()))
        for n in range(0, len(partners), 2):
            one, two = partners[n], partners[n + 1]
            left = jnp.concatenate([far_b[one][:, :48], far_b[two][:, :48]], axis=0)
            power = lax.dot_general(left, right, contract, preferred_element_type=jnp.float32)
            value = jnp.exp2(power)
            near = value.astype(jnp.bfloat16)
            rest = (value - near.astype(jnp.float32)).astype(jnp.bfloat16)
            acc = acc + lax.dot_general(
                jnp.concatenate([far_r[one], far_r[two]], axis=1),
                jnp.concatenate([near, rest], axis=1),
                contract,
                preferred_element_type=jnp.float32,
            )
        acc = acc[:, :slots] + acc[:, slots:]
        sums = acc[0:8] + acc[8:16]
        weight = rows_w[c + HALO][3:4]
        rows_f[c] = (PAIR_SCALE / ROOT) * weight * (own * sums[3:4] - sums)
        return carry

    lax.fori_loop(0, cells, one_cell, 0, unroll=4)

    for copy in copies_p:
        copy.wait_recv()
    moved = send_p[0]
    for d in range(1, beads):
        moved = moved + recv_p[d]
    for x in range(3):
        force = rows_f[:, x, :]
        frc_out[x] = force
        mom_out[x] = moved[x] + 0.25 * force

    for copy in copies_q + copies_p:
        copy.wait_send()

    @pl.when(has_high)
    def _():
        up_w.wait_send()
        up_r.wait_send()

    @pl.when(has_low)
    def _():
        down_w.wait_send()
        down_r.wait_send()


def per_device(positions, momenta, forces, noise, masses, strengths, cell_counts, neighbour_cells):
    beads = lax.axis_size("bead")
    spaces = lax.axis_size("space")
    cells, slots = masses.shape
    wide = cells + 2 * HALO
    coef, kicks = propagator(beads)
    block = (3, cells, slots)
    f32 = jnp.float32
    vmem = pl.BlockSpec(memory_space=pltpu.VMEM)
    smem = pl.BlockSpec(memory_space=pltpu.SMEM)
    out = pl.pallas_call(
        functools.partial(kernel, beads, spaces, coef),
        out_shape=[jax.ShapeDtypeStruct(block, f32)] * 3,
        in_specs=[smem] * 3 + [vmem] * 6,
        out_specs=[vmem] * 3,
        scratch_shapes=[
            pltpu.VMEM((beads,) + block, f32),
            pltpu.VMEM((beads,) + block, f32),
            pltpu.VMEM((beads,) + block, f32),
            pltpu.VMEM((beads,) + block, f32),
            pltpu.VMEM(block, f32),
            pltpu.VMEM((cells, slots), f32),
            pltpu.VMEM((3, HALO, slots), f32),
            pltpu.VMEM((HALO, slots), f32),
            pltpu.VMEM((3, HALO, slots), f32),
            pltpu.VMEM((HALO, slots), f32),
            pltpu.VMEM((wide, 8, slots), f32),
            pltpu.VMEM((cells, 8, slots), f32),
            pltpu.VMEM((wide, 8, slots), f32),
            pltpu.VMEM((wide + 1, slots, slots), jnp.bfloat16),
            pltpu.VMEM((wide + 1, 16, slots), jnp.bfloat16),
            pltpu.VMEM((cells, 8, slots), f32),
            pltpu.SemaphoreType.DMA((beads,)),
            pltpu.SemaphoreType.DMA((beads,)),
            pltpu.SemaphoreType.DMA((beads,)),
            pltpu.SemaphoreType.DMA((beads,)),
            pltpu.SemaphoreType.DMA((4,)),
            pltpu.SemaphoreType.DMA((4,)),
        ],
        compiler_params=pltpu.CompilerParams(
            collective_id=0, has_side_effects=True, vmem_limit_bytes=32 * 1024 * 1024
        ),
    )(
        jnp.asarray(kicks),
        cell_counts,
        neighbour_cells,
        positions[0],
        momenta[0],
        forces[0],
        noise[0],
        masses,
        strengths,
    )
    return tuple(x[None] for x in out)


def solution(mesh):
    whole = P(("groups", "bead"), None, "space", None)
    in_specs = (
        whole,
        whole,
        whole,
        whole,
        P(("groups", "space"), None),
        P(("groups", "space"), None),
        P("groups"),
        P(("groups", "space"), None),
    )
    return jax.shard_map(
        per_device, mesh=mesh, in_specs=in_specs, out_specs=(whole,) * 3, check_vma=False
    )
```

```python
import functools
import math

import jax
import jax.numpy as jnp
import numpy as np
from jax import lax
from jax.experimental import pallas as pl
from jax.experimental.pallas import tpu as pltpu
from jax.sharding import PartitionSpec as P

HALO = 16
TIME_STEP = 0.5
CYCLE_FREQ = 1.5
GAMMA_ZERO = 0.5
PAIR_SCALE = 0.005
ROOT = math.sqrt(math.log2(math.e))
MESH = pl.DeviceIdType.MESH


def modes_table(beads):
    k = np.arange(beads)[:, None]
    j = np.arange(beads)[None, :]
    angle = 2.0 * np.pi * (k * j % beads) / beads
    parity = np.where(j % 2 == 0, 1.0, -1.0)
    plain = np.ones_like(angle) / np.sqrt(beads)
    factor = np.sqrt(2.0 / beads)
    return np.where(
        k == 0,
        plain,
        np.where(
            k < beads // 2,
            factor * np.cos(angle),
            np.where(k == beads // 2, parity * plain, factor * np.sin(angle)),
        ),
    )


def propagator(beads):
    table = modes_table(beads)
    k = np.arange(beads)
    freq = 2.0 * CYCLE_FREQ * np.sin(np.pi * k / beads)
    half = 0.5 * TIME_STEP
    cos, sin = np.cos(freq * half), np.sin(freq * half)
    reach = np.where(k == 0, half, sin / np.where(k == 0, 1.0, freq))
    damp = np.exp(-np.where(k == 0, GAMMA_ZERO, 2.0 * freq) * TIME_STEP)
    kick = np.sqrt(1.0 - damp * damp)
    pull = -freq * sin
    modes = {
        "qq": cos * cos + reach * damp * pull,
        "qp": reach * cos * (1.0 + damp),
        "pq": pull * cos * (1.0 + damp),
        "pp": pull * reach + cos * cos * damp,
    }
    by_offset = {
        name: [float(np.sum(value * table[:, 0] * table[:, d])) for d in range(beads)]
        for name, value in modes.items()
    }
    noise = np.stack([(reach * kick)[:, None] * table, (cos * kick)[:, None] * table])
    return by_offset, noise.astype(np.float32)


def split3(value):
    high = value.astype(jnp.bfloat16).astype(jnp.float32)
    rest = value - high
    mid = rest.astype(jnp.bfloat16).astype(jnp.float32)
    return high, mid, rest - mid


def kernel(
    beads,
    spaces,
    coef,
    kicks_ref,
    counts_ref,
    list_ref,
    pos_ref,
    mom_ref,
    frc_ref,
    noi_ref,
    mass_ref,
    str_ref,
    pos_out,
    mom_out,
    frc_out,
    send_q,
    send_p,
    recv_q,
    recv_p,
    own_r,
    own_w,
    low_r,
    low_w,
    high_r,
    high_w,
    rows_v,
    rows_u,
    rows_w,
    far_b,
    far_r,
    rows_f,
    sq_sem,
    rq_sem,
    sp_sem,
    rp_sem,
    halo_send,
    halo_recv,
):
    bead = lax.axis_index("bead")
    space = lax.axis_index("space")
    cells, slots = mass_ref.shape
    neigh = list_ref.shape[1]
    wide = cells + 2 * HALO
    has_low = space > 0
    has_high = space < spaces - 1

    barrier = pltpu.get_barrier_semaphore()
    for d in range(1, beads):
        pl.semaphore_signal(
            barrier, inc=1, device_id={"bead": lax.rem(bead + d, beads)}, device_id_type=MESH
        )

    @pl.when(has_low)
    def _():
        pl.semaphore_signal(barrier, inc=1, device_id={"space": space - 1}, device_id_type=MESH)

    @pl.when(has_high)
    def _():
        pl.semaphore_signal(barrier, inc=1, device_id={"space": space + 1}, device_id_type=MESH)

    mass = mass_ref[...][None]
    root_mass = jnp.sqrt(mass)
    q = pos_ref[...]
    p = mom_ref[...] + 0.25 * frc_ref[...]
    scaled_p = p / mass
    noise_q = noi_ref[...] / root_mass
    for d in range(beads):
        target = lax.rem(bead + d, beads)
        send_q[d] = coef["qq"][d] * q + coef["qp"][d] * scaled_p + kicks_ref[0, bead, target] * noise_q

    lane = lax.broadcasted_iota(jnp.int32, (1, slots), 1)
    for c in range(cells):
        count = counts_ref[space * cells + c]
        own_w[c : c + 1, :] = jnp.where(lane < count, str_ref[c : c + 1, :], 0.0)

    pl.semaphore_wait(
        barrier, beads - 1 + has_low.astype(jnp.int32) + has_high.astype(jnp.int32)
    )

    def bead_copy(source, target, send, recv, d):
        return pltpu.make_async_remote_copy(
            src_ref=source.at[d],
            dst_ref=target.at[d],
            send_sem=send.at[d],
            recv_sem=recv.at[d],
            device_id={"bead": lax.rem(bead + d, beads)},
            device_id_type=MESH,
        )

    def space_copy(source, target, index, peer):
        return pltpu.make_async_remote_copy(
            src_ref=source,
            dst_ref=target,
            send_sem=halo_send.at[index],
            recv_sem=halo_recv.at[index],
            device_id={"space": peer},
            device_id_type=MESH,
        )

    first = pl.ds(0, HALO)
    last = pl.ds(cells - HALO, HALO)
    up_w = space_copy(own_w.at[last], low_w, 0, space + 1)
    down_w = space_copy(own_w.at[first], high_w, 1, space - 1)
    up_r = space_copy(own_r.at[:, last], low_r, 2, space + 1)
    down_r = space_copy(own_r.at[:, first], high_r, 3, space - 1)
    copies_q = [bead_copy(send_q, recv_q, sq_sem, rq_sem, d) for d in range(1, beads)]
    copies_p = [bead_copy(send_p, recv_p, sp_sem, rp_sem, d) for d in range(1, beads)]
    for copy in copies_q:
        copy.start()

    @pl.when(has_high)
    def _():
        up_w.start()

    @pl.when(has_low)
    def _():
        down_w.start()

    mass_q = mass * q
    noise_p = noi_ref[...] * root_mass
    for d in range(beads):
        target = lax.rem(bead + d, beads)
        send_p[d] = coef["pq"][d] * mass_q + coef["pp"][d] * p + kicks_ref[1, bead, target] * noise_p

    @pl.when(jnp.logical_not(has_low))
    def _():
        low_r[...] = jnp.zeros_like(low_r)
        low_w[...] = jnp.zeros_like(low_w)

    @pl.when(jnp.logical_not(has_high))
    def _():
        high_r[...] = jnp.zeros_like(high_r)
        high_w[...] = jnp.zeros_like(high_w)

    rows_v[...] = jnp.zeros_like(rows_v)
    rows_u[...] = jnp.zeros_like(rows_u)
    rows_w[...] = jnp.zeros_like(rows_w)
    far_b[wide] = jnp.zeros(far_b.shape[1:], far_b.dtype)
    far_r[wide] = jnp.zeros(far_r.shape[1:], far_r.dtype)

    for copy in copies_q:
        copy.wait_recv()
    total = send_q[0]
    for d in range(1, beads):
        total = total + recv_q[d]
    own_r[...] = total
    pos_out[...] = total

    @pl.when(has_high)
    def _():
        up_r.start()

    @pl.when(has_low)
    def _():
        down_r.start()

    for copy in copies_p:
        copy.start()

    def place(start, size, coords, weights):
        scaled = ROOT * coords
        norm = -0.5 * (scaled[0] * scaled[0] + scaled[1] * scaled[1] + scaled[2] * scaled[2])
        region = pl.ds(start, size)
        for x in range(3):
            rows_v[region, x, :] = scaled[x]
            rows_w[region, x, :] = scaled[x] * weights
        rows_v[region, 3, :] = norm
        rows_v[region, 4, :] = jnp.ones_like(norm)
        rows_w[region, 3, :] = weights
        return scaled, norm

    def features(start, size):
        pad = jnp.zeros((slots - 48, slots), jnp.float32)

        def group_of(g, carry):
            group = pl.ds(pl.multiple_of(start + g * 8, 8), 8)
            high, mid, low = split3(rows_v[group])
            stacked = jnp.concatenate([high, high, mid, high, low, mid], axis=1)
            value = rows_w[group]
            near = value.astype(jnp.bfloat16).astype(jnp.float32)
            far_r[group] = jnp.concatenate([near, value - near], axis=1).astype(jnp.bfloat16)
            for i in range(8):
                turned = jnp.transpose(jnp.concatenate([stacked[i], pad], axis=0))
                far_b[start + g * 8 + i] = turned.astype(jnp.bfloat16)
            return carry

        lax.fori_loop(0, size // 8, group_of, 0, unroll=True)

    scaled, norm = place(HALO, cells, total, own_w[...])
    for x in range(3):
        rows_u[:, x, :] = scaled[x]
    rows_u[:, 3, :] = jnp.ones_like(norm)
    rows_u[:, 4, :] = norm
    features(HALO, cells)

    @pl.when(has_low)
    def _():
        up_w.wait_recv()
        up_r.wait_recv()

    @pl.when(has_high)
    def _():
        down_w.wait_recv()
        down_r.wait_recv()

    place(0, HALO, low_r[...], low_w[...])
    features(0, HALO)
    place(HALO + cells, HALO, high_r[...], high_w[...])
    features(HALO + cells, HALO)

    def one_cell(c, carry):
        own = rows_u[c]
        high, mid, low = split3(own)
        right = jnp.concatenate([high, mid, high, low, high, mid], axis=0).astype(jnp.bfloat16)
        partners = [c + HALO]
        for n in range(neigh):
            entry = list_ref[c, n]
            local = jnp.clip(entry - space * cells + HALO, 0, wide - 1)
            partners.append(jnp.where(entry >= 0, local, wide))
        if len(partners) % 2:
            partners.append(wide)
        acc = jnp.zeros((16, 2 * slots), jnp.float32)
        contract = (((1,), (0,)), ((), ()))
        for n in range(0, len(partners), 2):
            one, two = partners[n], partners[n + 1]
            left = jnp.concatenate([far_b[one][:, :48], far_b[two][:, :48]], axis=0)
            power = lax.dot_general(left, right, contract, preferred_element_type=jnp.float32)
            value = jnp.exp2(power)
            near = value.astype(jnp.bfloat16)
            rest = (value - near.astype(jnp.float32)).astype(jnp.bfloat16)
            acc = acc + lax.dot_general(
                jnp.concatenate([far_r[one], far_r[two]], axis=1),
                jnp.concatenate([near, rest], axis=1),
                contract,
                preferred_element_type=jnp.float32,
            )
        acc = acc[:, :slots] + acc[:, slots:]
        sums = acc[0:8] + acc[8:16]
        weight = rows_w[c + HALO][3:4]
        rows_f[c] = (PAIR_SCALE / ROOT) * weight * (own * sums[3:4] - sums)
        return carry

    lax.fori_loop(0, cells, one_cell, 0, unroll=4)

    for copy in copies_p:
        copy.wait_recv()
    moved = send_p[0]
    for d in range(1, beads):
        moved = moved + recv_p[d]
    for x in range(3):
        force = rows_f[:, x, :]
        frc_out[x] = force
        mom_out[x] = moved[x] + 0.25 * force

    for copy in copies_q + copies_p:
        copy.wait_send()

    @pl.when(has_high)
    def _():
        up_w.wait_send()
        up_r.wait_send()

    @pl.when(has_low)
    def _():
        down_w.wait_send()
        down_r.wait_send()


def per_device(positions, momenta, forces, noise, masses, strengths, cell_counts, neighbour_cells):
    beads = lax.axis_size("bead")
    spaces = lax.axis_size("space")
    cells, slots = masses.shape
    wide = cells + 2 * HALO
    coef, kicks = propagator(beads)
    block = (3, cells, slots)
    f32 = jnp.float32
    vmem = pl.BlockSpec(memory_space=pltpu.VMEM)
    smem = pl.BlockSpec(memory_space=pltpu.SMEM)
    out = pl.pallas_call(
        functools.partial(kernel, beads, spaces, coef),
        out_shape=[jax.ShapeDtypeStruct(block, f32)] * 3,
        in_specs=[smem] * 3 + [vmem] * 6,
        out_specs=[vmem] * 3,
        scratch_shapes=[
            pltpu.VMEM((beads,) + block, f32),
            pltpu.VMEM((beads,) + block, f32),
            pltpu.VMEM((beads,) + block, f32),
            pltpu.VMEM((beads,) + block, f32),
            pltpu.VMEM(block, f32),
            pltpu.VMEM((cells, slots), f32),
            pltpu.VMEM((3, HALO, slots), f32),
            pltpu.VMEM((HALO, slots), f32),
            pltpu.VMEM((3, HALO, slots), f32),
            pltpu.VMEM((HALO, slots), f32),
            pltpu.VMEM((wide, 8, slots), f32),
            pltpu.VMEM((cells, 8, slots), f32),
            pltpu.VMEM((wide, 8, slots), f32),
            pltpu.VMEM((wide + 1, slots, slots), jnp.bfloat16),
            pltpu.VMEM((wide + 1, 16, slots), jnp.bfloat16),
            pltpu.VMEM((cells, 8, slots), f32),
            pltpu.SemaphoreType.DMA((beads,)),
            pltpu.SemaphoreType.DMA((beads,)),
            pltpu.SemaphoreType.DMA((beads,)),
            pltpu.SemaphoreType.DMA((beads,)),
            pltpu.SemaphoreType.DMA((4,)),
            pltpu.SemaphoreType.DMA((4,)),
        ],
        compiler_params=pltpu.CompilerParams(
            collective_id=0, has_side_effects=True, vmem_limit_bytes=32 * 1024 * 1024
        ),
    )(
        jnp.asarray(kicks),
        cell_counts,
        neighbour_cells,
        positions[0],
        momenta[0],
        forces[0],
        noise[0],
        masses,
        strengths,
    )
    return tuple(x[None] for x in out)


def solution(mesh):
    whole = P(("groups", "bead"), None, "space", None)
    in_specs = (
        whole,
        whole,
        whole,
        whole,
        P(("groups", "space"), None),
        P(("groups", "space"), None),
        P("groups"),
        P(("groups", "space"), None),
    )
    return jax.shard_map(
        per_device, mesh=mesh, in_specs=in_specs, out_specs=(whole,) * 3, check_vma=False
    )
```

```python
import functools
import math

import jax
import jax.numpy as jnp
import numpy as np
from jax import lax
from jax.experimental import pallas as pl
from jax.experimental.pallas import tpu as pltpu
from jax.sharding import PartitionSpec as P

HALO = 16
TIME_STEP = 0.5
CYCLE_FREQ = 1.5
GAMMA_ZERO = 0.5
PAIR_SCALE = 0.005
ROOT = math.sqrt(math.log2(math.e))
MESH = pl.DeviceIdType.MESH


def modes_table(beads):
    k = np.arange(beads)[:, None]
    j = np.arange(beads)[None, :]
    angle = 2.0 * np.pi * (k * j % beads) / beads
    parity = np.where(j % 2 == 0, 1.0, -1.0)
    plain = np.ones_like(angle) / np.sqrt(beads)
    factor = np.sqrt(2.0 / beads)
    return np.where(
        k == 0,
        plain,
        np.where(
            k < beads // 2,
            factor * np.cos(angle),
            np.where(k == beads // 2, parity * plain, factor * np.sin(angle)),
        ),
    )


def propagator(beads):
    table = modes_table(beads)
    k = np.arange(beads)
    freq = 2.0 * CYCLE_FREQ * np.sin(np.pi * k / beads)
    half = 0.5 * TIME_STEP
    cos, sin = np.cos(freq * half), np.sin(freq * half)
    reach = np.where(k == 0, half, sin / np.where(k == 0, 1.0, freq))
    damp = np.exp(-np.where(k == 0, GAMMA_ZERO, 2.0 * freq) * TIME_STEP)
    kick = np.sqrt(1.0 - damp * damp)
    pull = -freq * sin
    modes = {
        "qq": cos * cos + reach * damp * pull,
        "qp": reach * cos * (1.0 + damp),
        "pq": pull * cos * (1.0 + damp),
        "pp": pull * reach + cos * cos * damp,
    }
    by_offset = {
        name: [float(np.sum(value * table[:, 0] * table[:, d])) for d in range(beads)]
        for name, value in modes.items()
    }
    noise = np.stack([(reach * kick)[:, None] * table, (cos * kick)[:, None] * table])
    return by_offset, noise.astype(np.float32)


def split3(value):
    high = value.astype(jnp.bfloat16).astype(jnp.float32)
    rest = value - high
    mid = rest.astype(jnp.bfloat16).astype(jnp.float32)
    return high, mid, rest - mid


def kernel(
    beads,
    spaces,
    coef,
    kicks_ref,
    counts_ref,
    list_ref,
    pos_ref,
    mom_ref,
    frc_ref,
    noi_ref,
    mass_ref,
    str_ref,
    pos_out,
    mom_out,
    frc_out,
    send_q,
    send_p,
    recv_q,
    recv_p,
    own_r,
    own_w,
    low_r,
    low_w,
    high_r,
    high_w,
    rows_v,
    rows_u,
    rows_w,
    far_b,
    far_r,
    rows_f,
    sq_sem,
    rq_sem,
    sp_sem,
    rp_sem,
    halo_send,
    halo_recv,
):
    bead = lax.axis_index("bead")
    space = lax.axis_index("space")
    cells, slots = mass_ref.shape
    neigh = list_ref.shape[1]
    wide = cells + 2 * HALO
    has_low = space > 0
    has_high = space < spaces - 1

    barrier = pltpu.get_barrier_semaphore()
    for d in range(1, beads):
        pl.semaphore_signal(
            barrier, inc=1, device_id={"bead": lax.rem(bead + d, beads)}, device_id_type=MESH
        )

    @pl.when(has_low)
    def _():
        pl.semaphore_signal(barrier, inc=1, device_id={"space": space - 1}, device_id_type=MESH)

    @pl.when(has_high)
    def _():
        pl.semaphore_signal(barrier, inc=1, device_id={"space": space + 1}, device_id_type=MESH)

    mass = mass_ref[...][None]
    root_mass = jnp.sqrt(mass)
    q = pos_ref[...]
    p = mom_ref[...] + 0.25 * frc_ref[...]
    scaled_p = p / mass
    noise_q = noi_ref[...] / root_mass
    for d in range(beads):
        target = lax.rem(bead + d, beads)
        send_q[d] = coef["qq"][d] * q + coef["qp"][d] * scaled_p + kicks_ref[0, bead, target] * noise_q

    lane = lax.broadcasted_iota(jnp.int32, (1, slots), 1)
    for c in range(cells):
        count = counts_ref[space * cells + c]
        own_w[c : c + 1, :] = jnp.where(lane < count, str_ref[c : c + 1, :], 0.0)

    pl.semaphore_wait(
        barrier, beads - 1 + has_low.astype(jnp.int32) + has_high.astype(jnp.int32)
    )

    def bead_copy(source, target, send, recv, d):
        return pltpu.make_async_remote_copy(
            src_ref=source.at[d],
            dst_ref=target.at[d],
            send_sem=send.at[d],
            recv_sem=recv.at[d],
            device_id={"bead": lax.rem(bead + d, beads)},
            device_id_type=MESH,
        )

    def space_copy(source, target, index, peer):
        return pltpu.make_async_remote_copy(
            src_ref=source,
            dst_ref=target,
            send_sem=halo_send.at[index],
            recv_sem=halo_recv.at[index],
            device_id={"space": peer},
            device_id_type=MESH,
        )

    first = pl.ds(0, HALO)
    last = pl.ds(cells - HALO, HALO)
    up_w = space_copy(own_w.at[last], low_w, 0, space + 1)
    down_w = space_copy(own_w.at[first], high_w, 1, space - 1)
    up_r = space_copy(own_r.at[:, last], low_r, 2, space + 1)
    down_r = space_copy(own_r.at[:, first], high_r, 3, space - 1)
    copies_q = [bead_copy(send_q, recv_q, sq_sem, rq_sem, d) for d in range(1, beads)]
    copies_p = [bead_copy(send_p, recv_p, sp_sem, rp_sem, d) for d in range(1, beads)]
    for copy in copies_q:
        copy.start()

    @pl.when(has_high)
    def _():
        up_w.start()

    @pl.when(has_low)
    def _():
        down_w.start()

    mass_q = mass * q
    noise_p = noi_ref[...] * root_mass
    for d in range(beads):
        target = lax.rem(bead + d, beads)
        send_p[d] = coef["pq"][d] * mass_q + coef["pp"][d] * p + kicks_ref[1, bead, target] * noise_p

    @pl.when(jnp.logical_not(has_low))
    def _():
        low_r[...] = jnp.zeros_like(low_r)
        low_w[...] = jnp.zeros_like(low_w)

    @pl.when(jnp.logical_not(has_high))
    def _():
        high_r[...] = jnp.zeros_like(high_r)
        high_w[...] = jnp.zeros_like(high_w)

    rows_v[...] = jnp.zeros_like(rows_v)
    rows_u[...] = jnp.zeros_like(rows_u)
    rows_w[...] = jnp.zeros_like(rows_w)
    far_b[wide] = jnp.zeros(far_b.shape[1:], far_b.dtype)
    far_r[wide] = jnp.zeros(far_r.shape[1:], far_r.dtype)

    for copy in copies_q:
        copy.wait_recv()
    total = send_q[0]
    for d in range(1, beads):
        total = total + recv_q[d]
    own_r[...] = total
    pos_out[...] = total

    @pl.when(has_high)
    def _():
        up_r.start()

    @pl.when(has_low)
    def _():
        down_r.start()

    for copy in copies_p:
        copy.start()

    def place(start, size, coords, weights):
        scaled = ROOT * coords
        norm = -0.5 * (scaled[0] * scaled[0] + scaled[1] * scaled[1] + scaled[2] * scaled[2])
        region = pl.ds(start, size)
        for x in range(3):
            rows_v[region, x, :] = scaled[x]
            rows_w[region, x, :] = scaled[x] * weights
        rows_v[region, 3, :] = norm
        rows_v[region, 4, :] = jnp.ones_like(norm)
        rows_w[region, 3, :] = weights
        return scaled, norm

    def features(start, size):
        pad = jnp.zeros((slots - 48, slots), jnp.float32)

        def group_of(g, carry):
            group = pl.ds(pl.multiple_of(start + g * 8, 8), 8)
            high, mid, low = split3(rows_v[group])
            stacked = jnp.concatenate([high, high, mid, high, low, mid], axis=1)
            value = rows_w[group]
            near = value.astype(jnp.bfloat16).astype(jnp.float32)
            far_r[group] = jnp.concatenate([near, value - near], axis=1).astype(jnp.bfloat16)
            for i in range(8):
                turned = jnp.transpose(jnp.concatenate([stacked[i], pad], axis=0))
                far_b[start + g * 8 + i] = turned.astype(jnp.bfloat16)
            return carry

        lax.fori_loop(0, size // 8, group_of, 0, unroll=True)

    scaled, norm = place(HALO, cells, total, own_w[...])
    for x in range(3):
        rows_u[:, x, :] = scaled[x]
    rows_u[:, 3, :] = jnp.ones_like(norm)
    rows_u[:, 4, :] = norm
    features(HALO, cells)

    @pl.when(has_low)
    def _():
        up_w.wait_recv()
        up_r.wait_recv()

    @pl.when(has_high)
    def _():
        down_w.wait_recv()
        down_r.wait_recv()

    place(0, HALO, low_r[...], low_w[...])
    features(0, HALO)
    place(HALO + cells, HALO, high_r[...], high_w[...])
    features(HALO + cells, HALO)

    def one_cell(c, carry):
        own = rows_u[c]
        high, mid, low = split3(own)
        right = jnp.concatenate([high, mid, high, low, high, mid], axis=0).astype(jnp.bfloat16)
        partners = [c + HALO]
        for n in range(neigh):
            entry = list_ref[c, n]
            local = jnp.clip(entry - space * cells + HALO, 0, wide - 1)
            partners.append(jnp.where(entry >= 0, local, wide))
        if len(partners) % 2:
            partners.append(wide)
        acc = jnp.zeros((16, 2 * slots), jnp.float32)
        contract = (((1,), (0,)), ((), ()))
        for n in range(0, len(partners), 2):
            one, two = partners[n], partners[n + 1]
            left = jnp.concatenate([far_b[one][:, :48], far_b[two][:, :48]], axis=0)
            power = lax.dot_general(left, right, contract, preferred_element_type=jnp.float32)
            value = jnp.exp2(power)
            near = value.astype(jnp.bfloat16)
            rest = (value - near.astype(jnp.float32)).astype(jnp.bfloat16)
            acc = acc + lax.dot_general(
                jnp.concatenate([far_r[one], far_r[two]], axis=1),
                jnp.concatenate([near, rest], axis=1),
                contract,
                preferred_element_type=jnp.float32,
            )
        acc = acc[:, :slots] + acc[:, slots:]
        sums = acc[0:8] + acc[8:16]
        weight = rows_w[c + HALO][3:4]
        rows_f[c] = (PAIR_SCALE / ROOT) * weight * (own * sums[3:4] - sums)
        return carry

    lax.fori_loop(0, cells, one_cell, 0, unroll=8)

    for copy in copies_p:
        copy.wait_recv()
    moved = send_p[0]
    for d in range(1, beads):
        moved = moved + recv_p[d]
    for x in range(3):
        force = rows_f[:, x, :]
        frc_out[x] = force
        mom_out[x] = moved[x] + 0.25 * force

    for copy in copies_q + copies_p:
        copy.wait_send()

    @pl.when(has_high)
    def _():
        up_w.wait_send()
        up_r.wait_send()

    @pl.when(has_low)
    def _():
        down_w.wait_send()
        down_r.wait_send()


def per_device(positions, momenta, forces, noise, masses, strengths, cell_counts, neighbour_cells):
    beads = lax.axis_size("bead")
    spaces = lax.axis_size("space")
    cells, slots = masses.shape
    wide = cells + 2 * HALO
    coef, kicks = propagator(beads)
    block = (3, cells, slots)
    f32 = jnp.float32
    vmem = pl.BlockSpec(memory_space=pltpu.VMEM)
    smem = pl.BlockSpec(memory_space=pltpu.SMEM)
    out = pl.pallas_call(
        functools.partial(kernel, beads, spaces, coef),
        out_shape=[jax.ShapeDtypeStruct(block, f32)] * 3,
        in_specs=[smem] * 3 + [vmem] * 6,
        out_specs=[vmem] * 3,
        scratch_shapes=[
            pltpu.VMEM((beads,) + block, f32),
            pltpu.VMEM((beads,) + block, f32),
            pltpu.VMEM((beads,) + block, f32),
            pltpu.VMEM((beads,) + block, f32),
            pltpu.VMEM(block, f32),
            pltpu.VMEM((cells, slots), f32),
            pltpu.VMEM((3, HALO, slots), f32),
            pltpu.VMEM((HALO, slots), f32),
            pltpu.VMEM((3, HALO, slots), f32),
            pltpu.VMEM((HALO, slots), f32),
            pltpu.VMEM((wide, 8, slots), f32),
            pltpu.VMEM((cells, 8, slots), f32),
            pltpu.VMEM((wide, 8, slots), f32),
            pltpu.VMEM((wide + 1, slots, slots), jnp.bfloat16),
            pltpu.VMEM((wide + 1, 16, slots), jnp.bfloat16),
            pltpu.VMEM((cells, 8, slots), f32),
            pltpu.SemaphoreType.DMA((beads,)),
            pltpu.SemaphoreType.DMA((beads,)),
            pltpu.SemaphoreType.DMA((beads,)),
            pltpu.SemaphoreType.DMA((beads,)),
            pltpu.SemaphoreType.DMA((4,)),
            pltpu.SemaphoreType.DMA((4,)),
        ],
        compiler_params=pltpu.CompilerParams(
            collective_id=0, has_side_effects=True, vmem_limit_bytes=32 * 1024 * 1024
        ),
    )(
        jnp.asarray(kicks),
        cell_counts,
        neighbour_cells,
        positions[0],
        momenta[0],
        forces[0],
        noise[0],
        masses,
        strengths,
    )
    return tuple(x[None] for x in out)


def solution(mesh):
    whole = P(("groups", "bead"), None, "space", None)
    in_specs = (
        whole,
        whole,
        whole,
        whole,
        P(("groups", "space"), None),
        P(("groups", "space"), None),
        P("groups"),
        P(("groups", "space"), None),
    )
    return jax.shard_map(
        per_device, mesh=mesh, in_specs=in_specs, out_specs=(whole,) * 3, check_vma=False
    )
```
